256 devices in a mesh: grid: 32 (over z, y), tile: 8 (over x, core).
Axes of the slice: x: 4, y: 4, z: 8, core: 2. Of those that a mesh axis runs over, the one named last changes fastest.
Arguments:
- point_values: bfloat16 [1024, 16384], P('grid', 'tile'), may hold values from -1.75 to 1.75
- sig_blocks: int32 [32, 16], P('grid'), may hold values from 0 to 31, as said below
- density: bfloat16 [16384, 16384], P('grid', 'tile'), may hold values from -0.0625 to 0.0625
- coulomb_core: bfloat16 [512, 512], replicated, may hold values from -0.25 to 0.25
- screen_mask: int32 [32, 32], replicated, may hold values 0 or 1
- ao_centers: float32 [3, 16384], replicated, may hold values from -1 to 1
- ao_widths: float32 [16384], replicated, may hold values from 0.25 to 1
- point_coords: float32 [3, 1024], P(None, 'grid'), may hold values from -1 to 1
- lmo_coeffs: bfloat16 [16384, 2048], P('tile'), may hold values from -0.0625 to 0.0625
- domain_blocks: int32 [8, 16], replicated, may hold values from 0 to 31, as said below
Outputs:
- half: bfloat16 [2048, 16384], P('tile', 'grid')
The draws below stay inside these ranges and needn't reach their ends.
Inputs may be any that keep to these rules, and one draw needn't show every extreme that they name: `sig_blocks`: each batch names 16 different AO blocks. `domain_blocks`: each strip's 16 blocks are different, and every AO block lies in the domain of some strip.
All inputs are finite; a program needn't handle non-finite values.
Results may differ from the reference program's by a relative error of at most 0.02.
Values may be sent and summed in bfloat16 or wider, within the bound.
No kernel may reach another device: no remote copies, remote signals or barrier semaphores. Data moves between devices by JAX's collectives and lax.ppermute only.
A program may use at most 64 MiB of HBM per device.

```python
import math
import jax
import jax.numpy as jnp
from jax import lax

NAO = 16384
BLK = 512
BP = 32
LSTRIP = 256
DOMN = 16
BASIS_GROUP_NUM = 32
SIGN = 16
NBATCH = 32
POINTS = 1024
CT = 2048
NSTRIP = 8
NLMO = 2048
N_TILE = 8


def draw_sig_blocks(key, part):
    preferred_sequence = jax.random.permutation(jax.random.fold_in(key, 7), BASIS_GROUP_NUM)
    preference_increment = jnp.where(preferred_sequence < 4, 512, 0)
    raw_ranking_weights = jax.random.randint(jax.random.fold_in(key, 8), (NBATCH, BASIS_GROUP_NUM), 0, 1024)
    group_ranking_weights = (raw_ranking_weights + preference_increment[None, :]) * BASIS_GROUP_NUM + jnp.arange(BASIS_GROUP_NUM, dtype=jnp.int32)[None, :]
    return lax.top_k(group_ranking_weights, SIGN)[1].astype(jnp.int32)


def draw_domain_blocks(key, part):
    shuffled = jax.random.permutation(jax.random.fold_in(key, 9), BASIS_GROUP_NUM)
    window_starts = jnp.arange(NSTRIP, dtype=jnp.int32) * (BASIS_GROUP_NUM // NSTRIP)
    positions = (window_starts[:, None] + jnp.arange(DOMN, dtype=jnp.int32)[None, :]) % BASIS_GROUP_NUM
    return shuffled[positions].astype(jnp.int32)


def set_ends(drawn, own_key, low, largest):
    shape = drawn.shape
    place = [jax.random.randint(jax.random.fold_in(own_key, axis), (), 0, shape[axis]) for axis in range(len(shape))]
    drawn = drawn.at[tuple(place)].set(low)
    longest = shape.index(max(shape))
    place[longest] = (place[longest] + 1) % shape[longest]
    return drawn.at[tuple(place)].set(largest)


def block_scale(stream_key, extent, shards, low, high):
    factor_of = 1.0
    for position, parts in shards:
        draws = jax.random.uniform(jax.random.fold_in(jax.random.fold_in(stream_key, 6), position), (parts,), jnp.float32, low / len(shards), high / len(shards))
        factor_of = factor_of * jnp.repeat(jnp.exp(draws), extent[position] // parts).reshape((-1,) + (1,) * (len(extent) - 1 - position))
    return factor_of


def scatter_about(key, dims, width, bound, cuts=(), kind=jnp.bfloat16):
    result = width * jax.random.normal(key, dims, jnp.float32)
    if cuts:
        result = result * block_scale(key, dims, cuts, -0.22, 0.18)
    return jnp.clip(result, -bound, bound).astype(kind)


def setup_inputs(seed: int = 0) -> dict:
    seeds = jax.random.split(jax.random.key(seed), 11)
    return {
        "point_values": scatter_about(seeds[0], (POINTS, NAO), 0.3, 1.75, ((0, 32), (1, 8))),
        "sig_blocks": draw_sig_blocks(jax.random.fold_in(seeds[10], 71), 0),
        "density": scatter_about(seeds[2], (NAO, NAO), (SIGN * BLK) ** -0.5, 0.0625, ((0, 32), (1, 8))),
        "coulomb_core": scatter_about(seeds[3], (BLK, BLK), BLK ** -0.5, 0.25),
        "screen_mask": set_ends((jax.random.randint(seeds[4], (BASIS_GROUP_NUM, BASIS_GROUP_NUM), 0, 4) < 3).astype(jnp.int32), jax.random.fold_in(seeds[4], 1), 0, 1),
        "ao_centers": jnp.clip(jax.random.uniform(seeds[5], (3, NAO), jnp.float32, -1.0, 1.0), -1.0, 1.0),
        "ao_widths": jnp.clip(jnp.exp(jax.random.uniform(seeds[6], (NAO,), jnp.float32, math.log(0.25), math.log(1.0))), 0.25, 1.0),
        "point_coords": jnp.clip(jax.random.uniform(seeds[7], (3, POINTS), jnp.float32, -1.0, 1.0) * block_scale(seeds[7], (3, POINTS), ((1, 32),), -0.4, 0.0), -1.0, 1.0),
        "lmo_coeffs": scatter_about(seeds[8], (NAO, NLMO), (DOMN * BLK) ** -0.5, 0.0625, ((0, 8),)),
        "domain_blocks": draw_domain_blocks(jax.random.fold_in(seeds[10], 71), 0),
    }


highest = lax.Precision.HIGHEST

def batch_factors(values, block_list, coords, density_blocks, coulomb_core, screen_mask, ao_centers, ao_widths):
    sig_density = density_blocks[block_list][:, :, block_list, :].astype(jnp.float32)
    sig_values = values.reshape(BP, BASIS_GROUP_NUM, BLK)[:, block_list, :]
    per_column = jnp.einsum('kajc,pjc->jpka', sig_density, sig_values.astype(jnp.float32), precision=highest)
    owners = block_list // (CT // BLK)
    owner_onehot = (owners[:, None] == jnp.arange(N_TILE, dtype=jnp.int32)[None, :]).astype(jnp.float32)
    by_tile = jnp.einsum('jt,jpka->tpka', owner_onehot, per_column, precision=highest)
    rounded = lax.optimization_barrier(by_tile.astype(jnp.bfloat16)).astype(jnp.float32)
    density_term = lax.optimization_barrier(jnp.sum(rounded, axis=0))
    offsets = ao_centers[:, None, :] - coords[:, :, None]
    coefficient = 1.0 / jnp.sqrt(lax.optimization_barrier(jnp.sum(offsets * offsets, axis=0)) + ao_widths[None, :])
    sig_coeff = coefficient.reshape(BP, BASIS_GROUP_NUM, BLK)[:, block_list, :]
    weighted = sig_coeff * density_term
    screen = screen_mask[block_list][:, block_list].astype(jnp.float32)
    screened = jnp.einsum('kj,pja->pka', screen, weighted, precision=highest)
    mixed_term = jnp.einsum('ab,pkb->pka', coulomb_core.astype(jnp.float32), screened, precision=highest)
    potential = (sig_coeff * mixed_term).astype(jnp.bfloat16)
    return (sig_values, potential)

def reference(point_values, sig_blocks, density, coulomb_core, screen_mask, ao_centers, ao_widths, point_coords, lmo_coeffs, domain_blocks):
    density_blocks = density.reshape(BASIS_GROUP_NUM, BLK, BASIS_GROUP_NUM, BLK)
    values = point_values.reshape(NBATCH, BP, NAO)
    coords = jnp.transpose(point_coords.reshape(3, NBATCH, BP), (1, 0, 2))

    def one_batch(entries):
        return batch_factors(entries[0], entries[1], entries[2], density_blocks, coulomb_core, screen_mask, ao_centers, ao_widths)
    sig_values, potentials = lax.map(one_batch, (values, sig_blocks, coords))

    def accumulate(running_sum, entries):
        batch_values, batch_pots, block_list = entries
        tile_sum = jnp.einsum('pka,pjc->kjac', batch_values.astype(jnp.float32), batch_pots.astype(jnp.float32), precision=highest)
        return (running_sum.at[block_list[:, None], :, block_list[None, :], :].add(tile_sum), None)
    running_sum = jnp.zeros((BASIS_GROUP_NUM, BLK, BASIS_GROUP_NUM, BLK), jnp.float32)
    running_sum, unused = lax.scan(accumulate, running_sum, (sig_values, potentials, sig_blocks))
    exch_tile = running_sum.astype(jnp.bfloat16)
    strip_coeffs = jnp.transpose(lmo_coeffs.reshape(BASIS_GROUP_NUM, BLK, NSTRIP, LSTRIP), (2, 0, 1, 3))

    def one_strip(entries):
        coeff_strip, domain = entries
        exch_columns = exch_tile[:, :, domain, :].reshape(NAO, DOMN * BLK)
        coeff_rows = coeff_strip[domain].reshape(DOMN * BLK, LSTRIP)
        return lax.dot_general(coeff_rows, exch_columns, (((0,), (1,)), ((), ())), preferred_element_type=jnp.float32).astype(jnp.bfloat16)
    halves = lax.map(one_strip, (strip_coeffs, domain_blocks))
    return halves.reshape(NLMO, NAO)
```

```python
import jax
import jax.numpy as jnp
from jax import lax
from jax.sharding import PartitionSpec as P

NZ, NY, NT = 8, 4, 8
BP, BLK = 32, 512
bf16, f32 = jnp.bfloat16, jnp.float32


def gid(z, y):
    return (z % NZ) * NY + y % NY


def shift(x, dz, dy):
    pairs = [(gid(z, y), gid(z + dz, y + dy)) for z in range(NZ) for y in range(NY)]
    return lax.ppermute(x, "grid", pairs)


def put(buf, part, index):
    return lax.dynamic_update_slice_in_dim(buf, part[None], index, 0)


def ring(x, n, me, hop):
    buf = put(jnp.zeros((n,) + x.shape, x.dtype), x, me)
    up = down = x
    for s in range(1, (n - 1) // 2 + 1):
        up, down = hop(up, 1), hop(down, -1)
        buf = put(buf, up, (me - s) % n)
        buf = put(buf, down, (me + s) % n)
    h = x.shape[-2] // 2
    last = jnp.concatenate([hop(up[..., :h, :], 1), hop(down[..., h:, :], -1)], -2)
    return put(buf, last, (me + n // 2) % n)


def gather_grid(x, z, y):
    r, c = x.shape
    a, b = x[: r // 2], x[r // 2 :]
    a = ring(a, NY, y, lambda v, d: shift(v, 0, d))
    b = ring(b, NZ, z, lambda v, d: shift(v, d, 0))
    a = ring(a, NZ, z, lambda v, d: shift(v, d, 0))
    b = ring(b, NY, y, lambda v, d: shift(v, 0, d))
    return a, b


def shards(pv, sig, density, core, smask, centers, widths, coords, lmo, dom):
    g, j = lax.axis_index("grid"), lax.axis_index("tile")
    z, y = g // NY, g % NY
    nblk = smask.shape[0]
    ids = jnp.arange(nblk, dtype=jnp.int32)
    named = jnp.any(sig[0][:, None] == ids[None, :], axis=0).astype(f32)
    own = lax.dynamic_slice_in_dim(named, 4 * j, 4, 0)
    masked = pv * jnp.repeat(own, BLK)[None, :].astype(bf16)

    col = jnp.zeros((NY, BP, BLK), bf16)
    for s in range(NY):
        piece = lax.dynamic_slice_in_dim(masked, ((y + s) % NY) * BLK, BLK, 1)
        pairs = [
            (gid(a, b) * NT + t, gid(t, b + s) * NT + a)
            for a in range(NZ)
            for b in range(NY)
            for t in range(NT)
        ]
        piece = lax.ppermute(piece, ("grid", "tile"), pairs)
        col = put(col, piece, (y - s) % NY)
    x_col = lax.all_gather(col.reshape(NY * BP, BLK), "tile", axis=0, tiled=True)

    xa, xb = gather_grid(masked, z, y)
    dot_t = lambda u, v: lax.dot_general(u, v, (((1,), (1,)), ((), ())), preferred_element_type=f32)
    ya = dot_t(xa.reshape(-1, pv.shape[1]), density).astype(bf16).reshape(NZ, NY, 4, 4, BLK)
    yb = dot_t(xb.reshape(-1, pv.shape[1]), density).astype(bf16).reshape(NY, NZ, 4, 4, BLK)
    parts = jnp.concatenate([ya.transpose(2, 0, 1, 3, 4), yb.transpose(2, 1, 0, 3, 4)], 0)
    parts = lax.all_to_all(parts.reshape(NT, 32, 4, BLK), "tile", 0, 0, tiled=True)
    term = jnp.sum(parts.astype(f32), axis=0).astype(bf16)
    term = lax.all_to_all(term, "grid", 0, 0, tiled=True)

    pts = lax.dynamic_slice_in_dim(coords, 4 * j, 4, 1)
    off = centers[:, None, :] - pts[:, :, None]
    coef = 1.0 / jnp.sqrt(jnp.sum(off * off, axis=0) + widths[None, :])
    coef = coef.reshape(4, nblk, BLK).transpose(1, 0, 2) * named[:, None, None]
    weighted = (coef * term.astype(f32)).astype(bf16)
    screened = jnp.einsum("kj,jpa->kpa", smask.astype(bf16), weighted, preferred_element_type=f32)
    mixed = jnp.einsum("kpc,ac->kpa", screened.astype(bf16), core, preferred_element_type=f32)
    pot = (coef * mixed).astype(bf16)
    pot = lax.all_to_all(pot.reshape(NT, 4, 4, BLK), "tile", 0, 0, tiled=True)
    pot = pot.transpose(0, 2, 1, 3).reshape(BP, pv.shape[1])

    local_ids = 4 * j + jnp.arange(4, dtype=jnp.int32)
    in_dom = jnp.any(dom[:, :, None] == local_ids[None, None, :], axis=1).T.astype(bf16)
    dmask = jnp.broadcast_to(in_dom[:, None, :, None], (4, BLK, NT, 256)).reshape(lmo.shape)
    w = jnp.dot(pot, lmo * dmask, preferred_element_type=f32).astype(bf16)
    w = w.reshape(BP, NT, 256).transpose(1, 0, 2)
    w = lax.all_to_all(w, "tile", 0, 0, tiled=True)
    w = jnp.sum(w.astype(f32), axis=0).astype(bf16)
    w_all = lax.all_to_all(jnp.broadcast_to(w[None], (32, BP, 256)), "grid", 0, 0, tiled=True)
    return lax.dot_general(
        w_all.reshape(-1, 256), x_col, (((0,), (0,)), ((), ())), preferred_element_type=f32
    ).astype(bf16)


def solution(mesh):
    in_specs = (
        P("grid", "tile"),
        P("grid", None),
        P("grid", "tile"),
        P(),
        P(),
        P(),
        P(),
        P(None, "grid"),
        P("tile", None),
        P(),
    )
    return jax.shard_map(
        shards, mesh=mesh, in_specs=in_specs, out_specs=P("tile", "grid"), check_vma=False
    )
```

```python
import jax
import jax.numpy as jnp
from jax import lax
from jax.sharding import PartitionSpec as P

NZ, NY, NT = 8, 4, 8
BP, BLK = 32, 512
QP = 4
bf16, f32 = jnp.bfloat16, jnp.float32
Y_GROUPS = [[z * NY + y for y in range(NY)] for z in range(NZ)]
tie = lax.optimization_barrier


def along_z(x, d):
    pairs = [(z * NY + y, (z + d) % NZ * NY + y) for z in range(NZ) for y in range(NY)]
    return lax.ppermute(x, "grid", pairs)


def permute_all(x, dest):
    pairs = []
    for z in range(NZ):
        for y in range(NY):
            for t in range(NT):
                a, b, c = dest(z, y, t)
                pairs.append(((z * NY + y) * NT + t, (a * NY + b) * NT + c))
    return lax.ppermute(x, ("grid", "tile"), pairs)


def spread(x, axis, n, groups=None):
    copies = jnp.broadcast_to(x[None], (n,) + x.shape)
    return lax.all_to_all(copies, axis, 0, 0, tiled=True, axis_index_groups=groups)


def dot(u, v, cu, cv):
    return lax.dot_general(u, v, (((cu,), (cv,)), ((), ())), preferred_element_type=f32)


def shards(pv, sig, density, core, smask, centers, widths, coords, lmo, dom):
    g, j = lax.axis_index("grid"), lax.axis_index("tile")
    z, y = g // NY, g % NY
    nblk = smask.shape[0]
    cols = pv.shape[1]
    ids = jnp.arange(nblk, dtype=jnp.int32)
    named = jnp.any(sig[0][:, None] == ids[None, :], axis=0).astype(f32)
    own = lax.dynamic_slice_in_dim(named, 4 * j, 4, 0)
    masked = pv * jnp.repeat(own, BLK)[None, :].astype(bf16)

    xy = spread(masked, "grid", NY, Y_GROUPS)
    info = jnp.concatenate([named, coords.reshape(-1)])[None]
    piece = lax.dynamic_slice_in_dim(xy, y * BLK, BLK, 2).reshape(NY * BP, BLK)

    parts = jnp.zeros((NZ, NY * BP, BLK), bf16)

    def put(parts, x, s, row=0):
        rows = dot(x.reshape(-1, cols), density, 1, 1).astype(bf16)
        return lax.dynamic_update_slice(parts, rows[None], ((z - s) % NZ, row, 0))

    up = down = xy
    parts = put(parts, xy, 0)
    for s in range(1, 4):
        up, down = along_z(up, 1), along_z(down, -1)
        if s == 1:
            info, up, down = tie((info, up, down))
            info = permute_all(info, lambda a, b, c: (2 * b + c // 4, c % 4, a))[0]
        if s == 3:
            piece, up, down = tie((piece, up, down))
            piece = permute_all(piece, lambda a, b, c: (c, b, a))
        parts = put(put(parts, up, s), down, -s)
    up, down = along_z(up[: NY // 2], 1), along_z(down[NY // 2 :], -1)
    parts = put(put(parts, up, 4), down, 4, NY * BP // 2)

    named = info[:nblk]
    pts = lax.dynamic_slice_in_dim(info[nblk:].reshape(3, BP), QP * (g % 8), QP, 1)
    off = centers.reshape(3, nblk, 1, BLK) - pts.reshape(3, 1, QP, 1)
    coef = 1.0 / jnp.sqrt(jnp.sum(off * off, axis=0) + widths.reshape(nblk, 1, BLK))
    coef = coef * named[:, None, None]

    local_ids = 4 * j + jnp.arange(4, dtype=jnp.int32)
    in_dom = jnp.any(dom[:, :, None] == local_ids[None, None, :], axis=1).T.astype(bf16)
    dmask = jnp.broadcast_to(in_dom[:, None, :, None], (4, BLK, NT, 256)).reshape(lmo.shape)
    region = lmo * dmask
    parts, coef, region = tie((parts, coef, region))

    parts = lax.all_to_all(parts, "tile", 0, 0, tiled=True)
    term = jnp.sum(parts.astype(f32), axis=0).astype(bf16).reshape(NZ * NY, QP, BLK)
    term = lax.all_to_all(term, "grid", 0, 0, tiled=True)

    weighted = (coef * term.astype(f32)).astype(bf16)
    screened = jnp.einsum("kj,jpa->kpa", smask.astype(bf16), weighted, preferred_element_type=f32)
    mixed = jnp.einsum("kpc,ac->kpa", screened.astype(bf16), core, preferred_element_type=f32)
    pot = (coef * mixed).astype(bf16)
    pot = lax.all_to_all(pot.reshape(NT, 4, QP, BLK), "tile", 0, 0, tiled=True)
    pot = pot.transpose(0, 2, 1, 3).reshape(NT * QP, cols)

    w = dot(pot, region, 1, 0).astype(bf16)
    w = w.reshape(NT * QP, NT, 256).transpose(1, 0, 2)
    w = lax.all_to_all(w, "tile", 0, 0, tiled=True)
    w = jnp.sum(w.astype(f32), axis=0).astype(bf16)
    w_all = spread(w, "grid", NZ * NY).reshape(-1, 256)

    x_col = lax.all_gather(piece, "tile", axis=0, tiled=True)
    x_col = x_col.reshape(NZ, NY, 8, QP, BLK).transpose(1, 2, 0, 3, 4).reshape(-1, BLK)
    return dot(w_all, x_col, 0, 0).astype(bf16)


def solution(mesh):
    in_specs = (
        P("grid", "tile"),
        P("grid", None),
        P("grid", "tile"),
        P(),
        P(),
        P(),
        P(),
        P(None, "grid"),
        P("tile", None),
        P(),
    )
    return jax.shard_map(
        shards, mesh=mesh, in_specs=in_specs, out_specs=P("tile", "grid"), check_vma=False
    )
```

```python
import jax
import jax.numpy as jnp
from jax import lax
from jax.sharding import PartitionSpec as P

NZ, NY, NT = 8, 4, 8
BP, BLK = 32, 512
QP = 4
bf16, f32 = jnp.bfloat16, jnp.float32
Y_GROUPS = [[z * NY + y for y in range(NY)] for z in range(NZ)]
tie = lax.optimization_barrier


def along_z(x, d):
    pairs = [(z * NY + y, (z + d) % NZ * NY + y) for z in range(NZ) for y in range(NY)]
    return lax.ppermute(x, "grid", pairs)


def permute_all(x, dest):
    pairs = []
    for z in range(NZ):
        for y in range(NY):
            for t in range(NT):
                a, b, c = dest(z, y, t)
                pairs.append(((z * NY + y) * NT + t, (a * NY + b) * NT + c))
    return lax.ppermute(x, ("grid", "tile"), pairs)


def spread(x, axis, n, groups=None):
    copies = jnp.broadcast_to(x[None], (n,) + x.shape)
    return lax.all_to_all(copies, axis, 0, 0, tiled=True, axis_index_groups=groups)


def dot(u, v, cu, cv):
    return lax.dot_general(u, v, (((cu,), (cv,)), ((), ())), preferred_element_type=f32)


def shards(pv, sig, density, core, smask, centers, widths, coords, lmo, dom):
    g, j = lax.axis_index("grid"), lax.axis_index("tile")
    z, y = g // NY, g % NY
    nblk = smask.shape[0]
    cols = pv.shape[1]
    ids = jnp.arange(nblk, dtype=jnp.int32)
    named = jnp.any(sig[0][:, None] == ids[None, :], axis=0).astype(f32)
    own = lax.dynamic_slice_in_dim(named, 4 * j, 4, 0)
    masked = pv * jnp.repeat(own, BLK)[None, :].astype(bf16)

    xy = spread(masked, "grid", NY, Y_GROUPS)
    info = jnp.concatenate([named, coords.reshape(-1)])[None]
    piece = lax.dynamic_slice_in_dim(xy, y * BLK, BLK, 2).reshape(NY * BP, BLK)

    parts = jnp.zeros((NZ, NY * BP, BLK), bf16)

    def put(parts, x, s, row=0):
        rows = dot(x.reshape(-1, cols), density, 1, 1).astype(bf16)
        return lax.dynamic_update_slice(parts, rows[None], ((z - s) % NZ, row, 0))

    up = down = xy
    parts = put(parts, xy, 0)
    for s in range(1, 4):
        up, down = along_z(up, 1), along_z(down, -1)
        if s == 1:
            info, up, down = tie((info, up, down))
            info = permute_all(info, lambda a, b, c: (2 * b + c // 4, c % 4, a))[0]
        if s == 1:
            piece, up, down = tie((piece, up, down))
            piece = permute_all(piece, lambda a, b, c: (c, b, a))
        parts = put(put(parts, up, s), down, -s)
    up, down = along_z(up[: NY // 2], 1), along_z(down[NY // 2 :], -1)
    parts = put(put(parts, up, 4), down, 4, NY * BP // 2)

    named = info[:nblk]
    pts = lax.dynamic_slice_in_dim(info[nblk:].reshape(3, BP), QP * (g % 8), QP, 1)
    off = centers.reshape(3, nblk, 1, BLK) - pts.reshape(3, 1, QP, 1)
    coef = 1.0 / jnp.sqrt(jnp.sum(off * off, axis=0) + widths.reshape(nblk, 1, BLK))
    coef = coef * named[:, None, None]

    x_col = lax.all_gather(piece, "tile", axis=0, tiled=True)
    x_col = x_col.reshape(NZ, NY, 8, QP, BLK).transpose(1, 2, 0, 3, 4).reshape(-1, BLK)
    parts, coef, x_col = tie((parts, coef, x_col))

    parts = lax.all_to_all(parts, "tile", 0, 0, tiled=True)
    term = jnp.sum(parts.astype(f32), axis=0).astype(bf16).reshape(NZ * NY, QP, BLK)
    term = lax.all_to_all(term, "grid", 0, 0, tiled=True)

    weighted = (coef * term.astype(f32)).astype(bf16)
    screened = jnp.einsum("kj,jpa->kpa", smask.astype(bf16), weighted, preferred_element_type=f32)
    mixed = jnp.einsum("kpc,ac->kpa", screened.astype(bf16), core, preferred_element_type=f32)
    pot = (coef * mixed).astype(bf16)
    pot = lax.all_to_all(pot.reshape(NT, 4, QP, BLK), "tile", 0, 0, tiled=True)
    pot = pot.transpose(0, 2, 1, 3).reshape(NT * QP, cols)

    local_ids = 4 * j + jnp.arange(4, dtype=jnp.int32)
    in_dom = jnp.any(dom[:, :, None] == local_ids[None, None, :], axis=1).astype(f32)
    w = jnp.zeros((NT * QP, NT, 256), f32)
    for k in range(4):
        rows = slice(k * BLK, (k + 1) * BLK)
        term = dot(pot[:, rows], lmo[rows], 1, 0).reshape(NT * QP, NT, 256)
        w = w + term * in_dom[:, k][None, :, None]
    w = w.astype(bf16).transpose(1, 0, 2)
    w = lax.all_to_all(w, "tile", 0, 0, tiled=True)
    w = jnp.sum(w.astype(f32), axis=0).astype(bf16)
    w_all = spread(w, "grid", NZ * NY).reshape(-1, 256)
    return dot(w_all, x_col, 0, 0).astype(bf16)


def solution(mesh):
    in_specs = (
        P("grid", "tile"),
        P("grid", None),
        P("grid", "tile"),
        P(),
        P(),
        P(),
        P(),
        P(None, "grid"),
        P("tile", None),
        P(),
    )
    return jax.shard_map(
        shards, mesh=mesh, in_specs=in_specs, out_specs=P("tile", "grid"), check_vma=False
    )
```

```python
import jax
import jax.numpy as jnp
from jax import lax
from jax.experimental import pallas as pl
from jax.experimental.pallas import tpu as pltpu
from jax.sharding import PartitionSpec as P

NZ, NY, NT = 8, 4, 8
BP, BLK = 32, 512
QP = 4
bf16, f32 = jnp.bfloat16, jnp.float32
Y_GROUPS = [[z * NY + y for y in range(NY)] for z in range(NZ)]
tie = lax.optimization_barrier


def along_z(x, d):
    pairs = [(z * NY + y, (z + d) % NZ * NY + y) for z in range(NZ) for y in range(NY)]
    return lax.ppermute(x, "grid", pairs)


def permute_all(x, dest):
    pairs = []
    for z in range(NZ):
        for y in range(NY):
            for t in range(NT):
                a, b, c = dest(z, y, t)
                pairs.append(((z * NY + y) * NT + t, (a * NY + b) * NT + c))
    return lax.ppermute(x, ("grid", "tile"), pairs)


def spread(x, axis, n, groups=None):
    copies = jnp.broadcast_to(x[None], (n,) + x.shape)
    return lax.all_to_all(copies, axis, 0, 0, tiled=True, axis_index_groups=groups)


def dot(u, v, cu, cv):
    return lax.dot_general(u, v, (((cu,), (cv,)), ((), ())), preferred_element_type=f32)


def region_kernel(flags, pot, lmo, out):
    strip = pl.program_id(0)
    acc = jnp.zeros(out.shape[1:], f32)
    for k in range(flags.shape[1]):
        rows = pl.ds(k * BLK, BLK)
        part = jnp.dot(pot[:, rows], lmo[rows, :], preferred_element_type=f32)
        acc = acc + jnp.where(flags[strip, k] != 0, part, 0.0)
    out[0] = acc.astype(out.dtype)


def region_product(flags, pot, lmo):
    strips = flags.shape[0]
    points, cols = pot.shape
    width = lmo.shape[1] // strips
    return pl.pallas_call(
        region_kernel,
        grid=(strips,),
        in_specs=[
            pl.BlockSpec(memory_space=pltpu.SMEM),
            pl.BlockSpec((points, cols), lambda i: (0, 0)),
            pl.BlockSpec((cols, width), lambda i: (0, i)),
        ],
        out_specs=pl.BlockSpec((1, points, width), lambda i: (i, 0, 0)),
        out_shape=jax.ShapeDtypeStruct((strips, points, width), bf16),
        compiler_params=pltpu.CompilerParams(vmem_limit_bytes=16 * 2**20),
        cost_estimate=pl.CostEstimate(
            flops=2 * points * cols * lmo.shape[1], bytes_accessed=2 * lmo.size, transcendentals=0
        ),
    )(flags, pot, lmo)


def shards(pv, sig, density, core, smask, centers, widths, coords, lmo, dom):
    g, j = lax.axis_index("grid"), lax.axis_index("tile")
    z, y = g // NY, g % NY
    nblk = smask.shape[0]
    cols = pv.shape[1]
    ids = jnp.arange(nblk, dtype=jnp.int32)
    named = jnp.any(sig[0][:, None] == ids[None, :], axis=0).astype(f32)
    own = lax.dynamic_slice_in_dim(named, 4 * j, 4, 0)
    masked = pv * jnp.repeat(own, BLK)[None, :].astype(bf16)

    xy = spread(masked, "grid", NY, Y_GROUPS)
    info = jnp.concatenate([named, coords.reshape(-1)])[None]
    piece = lax.dynamic_slice_in_dim(xy, y * BLK, BLK, 2)
    piece = piece.reshape(NT, NY, QP, BLK).transpose(1, 0, 2, 3).reshape(NY * BP, BLK)

    def product(x):
        rows = dot(x.reshape(-1, cols), density, 1, 1).astype(bf16)
        return rows.reshape(-1, 1, 16, BLK)

    def tile_sum(blocks):
        parts = jnp.concatenate(blocks, 1)
        parts = lax.all_to_all(parts, "tile", 0, 0, tiled=True)
        return jnp.sum(parts.astype(f32), axis=0).astype(bf16)

    blocks = {0: product(xy)}
    up = down = xy
    for s in range(1, 4):
        up, down = along_z(up, 1), along_z(down, -1)
        if s == 1:
            info, piece, up, down = tie((info, piece, up, down))
            info = permute_all(info, lambda a, b, c: (a, c // 2, 2 * b + c % 2))[0]
            piece = permute_all(piece, lambda a, b, c: (c, b, a))
        blocks[s], blocks[-s] = product(up), product(down)
        if s == 2:
            early = tile_sum([blocks[i] for i in (-2, -1, 0, 1, 2)])
    up, down = along_z(up[: NY // 2], 1), along_z(down[NY // 2 :], -1)
    blocks[4] = jnp.concatenate([product(up), product(down)], 0)
    x_col = lax.all_gather(piece, "tile", axis=0, tiled=True)

    named = info[:nblk]
    pts = lax.dynamic_slice_in_dim(info[nblk:].reshape(3, BP), 16 * (j % 2) + QP * y, QP, 1)
    off = centers.reshape(3, nblk, 1, BLK) - pts.reshape(3, 1, QP, 1)
    coef = 1.0 / jnp.sqrt(jnp.sum(off * off, axis=0) + widths.reshape(nblk, 1, BLK))
    coef = coef * named[:, None, None]
    blocks[4], coef, x_col = tie((blocks[4], coef, x_col))
    late = tile_sum([blocks[i] for i in (3, -3, 4)])

    around = [early[2], early[1], early[0], late[1], late[2], late[0], early[4], early[3]]
    term = lax.dynamic_slice_in_dim(jnp.stack(around + around), (NZ - z) % NZ, NZ, 0)
    term = lax.all_to_all(term.reshape(NZ * NY, QP, BLK), "grid", 0, 0, tiled=True)

    weighted = (coef * term.astype(f32)).astype(bf16)
    screened = jnp.einsum("kj,jpa->kpa", smask.astype(bf16), weighted, preferred_element_type=f32)
    mixed = jnp.einsum("kpc,ac->kpa", screened.astype(bf16), core, preferred_element_type=f32)
    pot = (coef * mixed).astype(bf16)
    pot = lax.all_to_all(pot.reshape(NT, 4, QP, BLK), "tile", 0, 0, tiled=True)
    pot = pot.transpose(0, 2, 1, 3).reshape(NT * QP, cols)

    local_ids = 4 * j + jnp.arange(4, dtype=jnp.int32)
    in_dom = jnp.any(dom[:, :, None] == local_ids[None, None, :], axis=1).astype(jnp.int32)
    w = region_product(in_dom, pot, lmo)
    w = lax.all_to_all(w, "tile", 0, 0, tiled=True)
    w = jnp.sum(w.astype(f32), axis=0).astype(bf16)
    w_all = spread(w, "grid", NZ * NY).reshape(-1, 256)
    return dot(w_all, x_col, 0, 0).astype(bf16)


def solution(mesh):
    in_specs = (
        P("grid", "tile"),
        P("grid", None),
        P("grid", "tile"),
        P(),
        P(),
        P(),
        P(),
        P(None, "grid"),
        P("tile", None),
        P(),
    )
    return jax.shard_map(
        shards, mesh=mesh, in_specs=in_specs, out_specs=P("tile", "grid"), check_vma=False
    )
```

```python
import jax
import jax.numpy as jnp
from jax import lax
from jax.experimental import pallas as pl
from jax.experimental.pallas import tpu as pltpu
from jax.sharding import PartitionSpec as P

NZ, NY, NT = 8, 4, 8
BP, BLK = 32, 512
QP = 4
bf16, f32 = jnp.bfloat16, jnp.float32
Y_GROUPS = [[z * NY + y for y in range(NY)] for z in range(NZ)]
tie = lax.optimization_barrier


def along_z(x, d):
    pairs = [(z * NY + y, (z + d) % NZ * NY + y) for z in range(NZ) for y in range(NY)]
    return lax.ppermute(x, "grid", pairs)


def permute_all(x, dest):
    pairs = []
    for z in range(NZ):
        for y in range(NY):
            for t in range(NT):
                a, b, c = dest(z, y, t)
                pairs.append(((z * NY + y) * NT + t, (a * NY + b) * NT + c))
    return lax.ppermute(x, ("grid", "tile"), pairs)


def spread(x, axis, n, groups=None):
    copies = jnp.broadcast_to(x[None], (n,) + x.shape)
    return lax.all_to_all(copies, axis, 0, 0, tiled=True, axis_index_groups=groups)


def dot(u, v, cu, cv):
    return lax.dot_general(u, v, (((cu,), (cv,)), ((), ())), preferred_element_type=f32)


def region_kernel(flags, pot, lmo, out, acc):
    step = pl.program_id(0)
    strips, _, width = acc.shape

    @pl.when(step == 0)
    def _():
        acc[...] = jnp.zeros_like(acc)

    for strip in range(strips):

        @pl.when(flags[strip, step * lmo.shape[0] // BLK] != 0)
        def _():
            part = lmo[:, strip * width : (strip + 1) * width]
            acc[strip] += jnp.dot(pot[...], part, preferred_element_type=f32)

    @pl.when(step == pl.num_programs(0) - 1)
    def _():
        out[...] = acc[...].astype(out.dtype)


def region_product(flags, pot, lmo, rows=256):
    strips = flags.shape[0]
    points, cols = pot.shape
    width = lmo.shape[1] // strips
    return pl.pallas_call(
        region_kernel,
        grid=(cols // rows,),
        in_specs=[
            pl.BlockSpec(memory_space=pltpu.SMEM),
            pl.BlockSpec((points, rows), lambda i: (0, i)),
            pl.BlockSpec((rows, lmo.shape[1]), lambda i: (i, 0)),
        ],
        out_specs=pl.BlockSpec((strips, points, width), lambda i: (0, 0, 0)),
        out_shape=jax.ShapeDtypeStruct((strips, points, width), bf16),
        scratch_shapes=[pltpu.VMEM((strips, points, width), f32)],
        compiler_params=pltpu.CompilerParams(vmem_limit_bytes=52 * 2**20),
        cost_estimate=pl.CostEstimate(
            flops=2 * points * cols * lmo.shape[1], bytes_accessed=2 * lmo.size, transcendentals=0
        ),
    )(flags, pot, lmo)


def place_kernel(z, parts, out):
    for m in range(NZ):
        total = jnp.sum(parts[:, m].astype(f32), axis=0).astype(out.dtype)
        out[pl.ds((z[0] + m) % NZ, 1)] = total[None]


def sum_and_place(z, parts):
    whole = pl.BlockSpec(memory_space=pltpu.VMEM)
    return pl.pallas_call(
        place_kernel,
        in_specs=[pl.BlockSpec(memory_space=pltpu.SMEM), whole],
        out_specs=whole,
        out_shape=jax.ShapeDtypeStruct(parts.shape[1:], bf16),
        cost_estimate=pl.CostEstimate(
            flops=parts.size, bytes_accessed=2 * parts.size, transcendentals=0
        ),
    )(z.reshape(1), parts)


def shards(pv, sig, density, core, smask, centers, widths, coords, lmo, dom):
    g, j = lax.axis_index("grid"), lax.axis_index("tile")
    z, y = g // NY, g % NY
    nblk = smask.shape[0]
    cols = pv.shape[1]
    ids = jnp.arange(nblk, dtype=jnp.int32)
    named = jnp.any(sig[0][:, None] == ids[None, :], axis=0).astype(f32)
    own = lax.dynamic_slice_in_dim(named, 4 * j, 4, 0)
    masked = pv * jnp.repeat(own, BLK)[None, :].astype(bf16)

    xy = spread(masked, "grid", NY, Y_GROUPS)
    info = jnp.concatenate([named, coords.reshape(-1)])[None]
    piece = lax.dynamic_slice_in_dim(xy, y * BLK, BLK, 2)
    piece = piece.reshape(NT, NY, QP, BLK).transpose(1, 0, 2, 3).reshape(NY * BP, BLK)

    def product(buf, x, slot, row=0):
        rows = dot(x.reshape(-1, cols), density, 1, 1).astype(bf16)
        return lax.dynamic_update_slice(buf, rows.reshape(-1, 1, 16, BLK), (row, slot, 0, 0))

    info = permute_all(info, lambda a, b, c: (a, c // 2, 2 * b + c % 2))[0]
    info, xy = tie((info, xy))
    parts = product(jnp.zeros((NT, NZ, 16, BLK), bf16), xy, 0)
    up = down = xy
    for s in range(1, 4):
        up, down = along_z(up, 1), along_z(down, -1)
        parts = product(parts, up, NZ - s)
        parts = product(parts, down, s)
    up, down = along_z(up[: NY // 2], 1), along_z(down[NY // 2 :], -1)
    parts = product(parts, up, 4)
    parts = product(parts, down, 4, NT // 2)

    named = info[:nblk]
    pts = lax.dynamic_slice_in_dim(info[nblk:].reshape(3, BP), 16 * (j % 2) + QP * y, QP, 1)
    off = centers.reshape(3, nblk, 1, BLK) - pts.reshape(3, 1, QP, 1)
    coef = 1.0 / jnp.sqrt(jnp.sum(off * off, axis=0) + widths.reshape(nblk, 1, BLK))
    coef = coef * named[:, None, None]
    parts, coef, piece = tie((parts, coef, piece))
    piece = permute_all(piece, lambda a, b, c: (c, b, a))
    parts = lax.all_to_all(parts, "tile", 0, 0, tiled=True)
    term = sum_and_place(z, parts).reshape(NZ * NY, QP, BLK)
    term, piece = tie((term, piece))
    x_col = lax.all_gather(piece, "tile", axis=0, tiled=True)
    term = lax.all_to_all(term, "grid", 0, 0, tiled=True)

    weighted = (coef * term.astype(f32)).astype(bf16)
    screened = jnp.einsum("kj,jpa->kpa", smask.astype(bf16), weighted, preferred_element_type=f32)
    mixed = jnp.einsum("kpc,ac->kpa", screened.astype(bf16), core, preferred_element_type=f32)
    pot = (coef * mixed).astype(bf16)
    pot = lax.all_to_all(pot.reshape(NT, 4, QP, BLK), "tile", 0, 0, tiled=True)
    pot = pot.transpose(0, 2, 1, 3).reshape(NT * QP, cols)

    local_ids = 4 * j + jnp.arange(4, dtype=jnp.int32)
    in_dom = jnp.any(dom[:, :, None] == local_ids[None, None, :], axis=1).astype(jnp.int32)
    w = region_product(in_dom, pot, lmo)
    w = lax.all_to_all(w, "tile", 0, 0, tiled=True)
    w = jnp.sum(w.astype(f32), axis=0).astype(bf16)
    w_all = spread(w, "grid", NZ * NY).reshape(-1, 256)
    return dot(w_all, x_col, 0, 0).astype(bf16)


def solution(mesh):
    in_specs = (
        P("grid", "tile"),
        P("grid", None),
        P("grid", "tile"),
        P(),
        P(),
        P(),
        P(),
        P(None, "grid"),
        P("tile", None),
        P(),
    )
    return jax.shard_map(
        shards, mesh=mesh, in_specs=in_specs, out_specs=P("tile", "grid"), check_vma=False
    )
```

```python
import jax
import jax.numpy as jnp
from jax import lax
from jax.experimental import pallas as pl
from jax.experimental.pallas import tpu as pltpu
from jax.sharding import PartitionSpec as P

NZ, NY, NT = 8, 4, 8
BP, BLK = 32, 512
QP = 4
bf16, f32 = jnp.bfloat16, jnp.float32
Y_GROUPS = [[z * NY + y for y in range(NY)] for z in range(NZ)]
tie = lax.optimization_barrier


def along_z(x, d):
    pairs = [(z * NY + y, (z + d) % NZ * NY + y) for z in range(NZ) for y in range(NY)]
    return lax.ppermute(x, "grid", pairs)


def permute_all(x, dest):
    pairs = []
    for z in range(NZ):
        for y in range(NY):
            for t in range(NT):
                a, b, c = dest(z, y, t)
                pairs.append(((z * NY + y) * NT + t, (a * NY + b) * NT + c))
    return lax.ppermute(x, ("grid", "tile"), pairs)


def spread(x, axis, n, groups=None):
    copies = jnp.broadcast_to(x[None], (n,) + x.shape)
    return lax.all_to_all(copies, axis, 0, 0, tiled=True, axis_index_groups=groups)


def dot(u, v, cu, cv):
    return lax.dot_general(u, v, (((cu,), (cv,)), ((), ())), preferred_element_type=f32)


def region_kernel(pot, lmo, keep, out, acc):
    step = pl.program_id(0)
    strips, _, width = out.shape

    @pl.when(step == 0)
    def _():
        acc[...] = jnp.zeros_like(acc)

    part = jnp.dot(pot[...], lmo[...], preferred_element_type=f32)
    acc[...] += jnp.where(keep[0] != 0, part, 0.0)

    @pl.when(step == pl.num_programs(0) - 1)
    def _():
        for strip in range(strips):
            out[strip] = acc[:, strip * width : (strip + 1) * width].astype(out.dtype)


def region_product(in_dom, pot, lmo, rows=256):
    strips, blocks = in_dom.shape
    points, cols = pot.shape
    wide = lmo.shape[1]
    keep = jnp.repeat(in_dom.T, wide // strips, axis=1).reshape(blocks, 1, wide)
    return pl.pallas_call(
        region_kernel,
        grid=(cols // rows,),
        in_specs=[
            pl.BlockSpec((points, rows), lambda i: (0, i)),
            pl.BlockSpec((rows, wide), lambda i: (i, 0)),
            pl.BlockSpec((1, 1, wide), lambda i: (i * rows // BLK, 0, 0)),
        ],
        out_specs=pl.BlockSpec((strips, points, wide // strips), lambda i: (0, 0, 0)),
        out_shape=jax.ShapeDtypeStruct((strips, points, wide // strips), bf16),
        scratch_shapes=[pltpu.VMEM((points, wide), f32)],
        compiler_params=pltpu.CompilerParams(vmem_limit_bytes=52 * 2**20),
        cost_estimate=pl.CostEstimate(
            flops=2 * points * cols * wide, bytes_accessed=2 * lmo.size, transcendentals=0
        ),
    )(pot, lmo, keep)


def place_kernel(z, early, late, out):
    for m in range(-2, 6):
        part = early[:, m + 2] if m < 3 else late[:, m - 3]
        total = jnp.sum(part.astype(f32), axis=0)
        first = (z[0] + m + NZ) % NZ * NY
        for q in range(NY):
            out[pl.ds(first + q, 1)] = total[q * QP : (q + 1) * QP].astype(out.dtype)[None]


def sum_and_place(z, early, late):
    whole = pl.BlockSpec(memory_space=pltpu.VMEM)
    return pl.pallas_call(
        place_kernel,
        in_specs=[pl.BlockSpec(memory_space=pltpu.SMEM), whole, whole],
        out_specs=whole,
        out_shape=jax.ShapeDtypeStruct((NZ * NY, QP, BLK), bf16),
        cost_estimate=pl.CostEstimate(
            flops=early.size, bytes_accessed=2 * early.size, transcendentals=0
        ),
    )(z.reshape(1), early, late)


def shards(pv, sig, density, core, smask, centers, widths, coords, lmo, dom):
    g, j = lax.axis_index("grid"), lax.axis_index("tile")
    z, y = g // NY, g % NY
    nblk = smask.shape[0]
    cols = pv.shape[1]
    ids = jnp.arange(nblk, dtype=jnp.int32)
    named = jnp.any(sig[0][:, None] == ids[None, :], axis=0).astype(f32)
    own = lax.dynamic_slice_in_dim(named, 4 * j, 4, 0)
    masked = pv * jnp.repeat(own, BLK)[None, :].astype(bf16)

    xy = spread(masked, "grid", NY, Y_GROUPS)
    info = jnp.concatenate([named, coords.reshape(-1)])[None]
    piece = lax.dynamic_slice_in_dim(xy, y * BLK, BLK, 2)
    piece = piece.reshape(NT, NY, QP, BLK).transpose(1, 0, 2, 3).reshape(NY * BP, BLK)

    def product(buf, x, slot, row=0):
        rows = dot(x.reshape(-1, cols), density, 1, 1).astype(bf16)
        return lax.dynamic_update_slice(buf, rows.reshape(-1, 1, 16, BLK), (row, slot, 0, 0))

    info = permute_all(info, lambda a, b, c: (a, c // 2, 2 * b + c % 2))[0]
    info, xy = tie((info, xy))
    over_tile = lambda v: lax.all_to_all(v, "tile", 0, 0, tiled=True)
    early = product(jnp.zeros((NT, 5, 16, BLK), bf16), xy, 2)
    late = jnp.zeros((NT, 3, 16, BLK), bf16)
    up = down = xy
    for s in range(1, 4):
        up, down = tie((along_z(up, 1), along_z(down, -1)))
        if s < 3:
            early = product(product(early, up, 2 - s), down, 2 + s)
        else:
            late = product(product(late, up, 2), down, 0)
    early = over_tile(early)
    up, down = along_z(up[: NY // 2], 1), along_z(down[NY // 2 :], -1)
    late = product(product(late, up, 1), down, 1, NT // 2)

    named = info[:nblk]
    pts = lax.dynamic_slice_in_dim(info[nblk:].reshape(3, BP), 16 * (j % 2) + QP * y, QP, 1)
    off = centers.reshape(3, nblk, 1, BLK) - pts.reshape(3, 1, QP, 1)
    coef = 1.0 / jnp.sqrt(jnp.sum(off * off, axis=0) + widths.reshape(nblk, 1, BLK))
    coef = coef * named[:, None, None]
    late, coef, piece = tie((late, coef, piece))
    piece = permute_all(piece, lambda a, b, c: (c, b, a))
    term = sum_and_place(z, early, over_tile(late))
    term, piece = tie((term, piece))
    x_col = lax.all_gather(piece, "tile", axis=0, tiled=True)
    term = lax.all_to_all(term, "grid", 0, 0, tiled=True)

    weighted = (coef * term.astype(f32)).astype(bf16)
    screened = jnp.einsum("kj,jpa->kpa", smask.astype(bf16), weighted, preferred_element_type=f32)
    mixed = jnp.einsum("kpc,ac->kpa", screened.astype(bf16), core, preferred_element_type=f32)
    pot = (coef * mixed).astype(bf16)
    pot = lax.all_to_all(pot.reshape(NT, 4, QP, BLK), "tile", 0, 0, tiled=True)
    pot = pot.transpose(0, 2, 1, 3).reshape(NT * QP, cols)

    local_ids = 4 * j + jnp.arange(4, dtype=jnp.int32)
    in_dom = jnp.any(dom[:, :, None] == local_ids[None, None, :], axis=1).astype(jnp.int32)
    w = region_product(in_dom, pot, lmo)
    w = lax.all_to_all(w, "tile", 0, 0, tiled=True)
    w = jnp.sum(w.astype(f32), axis=0).astype(bf16)
    w, x_col = tie((w, x_col))
    w_all = spread(w, "grid", NZ * NY).reshape(-1, 256)
    return dot(w_all, x_col, 0, 0).astype(bf16)


def solution(mesh):
    in_specs = (
        P("grid", "tile"),
        P("grid", None),
        P("grid", "tile"),
        P(),
        P(),
        P(),
        P(),
        P(None, "grid"),
        P("tile", None),
        P(),
    )
    return jax.shard_map(
        shards, mesh=mesh, in_specs=in_specs, out_specs=P("tile", "grid"), check_vma=False
    )
```

```python
import jax
import jax.numpy as jnp
from jax import lax
from jax.experimental import pallas as pl
from jax.experimental.pallas import tpu as pltpu
from jax.sharding import PartitionSpec as P

NZ, NY, NT = 8, 4, 8
BP, BLK = 32, 512
QP = 4
LEAD = 1
bf16, f32 = jnp.bfloat16, jnp.float32
Y_GROUPS = [[z * NY + y for y in range(NY)] for z in range(NZ)]
tie = lax.optimization_barrier


def along_z(x, d):
    pairs = [(z * NY + y, (z + d) % NZ * NY + y) for z in range(NZ) for y in range(NY)]
    return lax.ppermute(x, "grid", pairs)


def permute_all(x, dest):
    pairs = []
    for z in range(NZ):
        for y in range(NY):
            for t in range(NT):
                a, b, c = dest(z, y, t)
                pairs.append(((z * NY + y) * NT + t, (a * NY + b) * NT + c))
    return lax.ppermute(x, ("grid", "tile"), pairs)


def spread(x, axis, n):
    copies = jnp.broadcast_to(x[None], (n,) + x.shape)
    return lax.all_to_all(copies, axis, 0, 0, tiled=True)


def dot(u, v, cu, cv):
    return lax.dot_general(u, v, (((cu,), (cv,)), ((), ())), preferred_element_type=f32)


def region_kernel(*refs):
    pots, lmos, keep, out, acc = refs[:4], refs[4:8], refs[8], refs[9], refs[10]
    step = pl.program_id(0)
    strips, _, width = out.shape

    @pl.when(step == 0)
    def _():
        acc[...] = jnp.zeros_like(acc)

    total = acc[...]
    for k in range(4):
        part = jnp.dot(pots[k][...], lmos[k][...], preferred_element_type=f32)
        total = total + jnp.where(keep[k] != 0, part, 0.0)
    acc[...] = total

    @pl.when(step == pl.num_programs(0) - 1)
    def _():
        for strip in range(strips):
            out[strip] = acc[:, strip * width : (strip + 1) * width].astype(out.dtype)


def region_product(in_dom, pot, lmo, rows=128):
    strips, blocks = in_dom.shape
    points, cols = pot.shape
    wide = lmo.shape[1]
    keep = jnp.repeat(in_dom.T, wide // strips, axis=1).reshape(blocks, 1, wide)
    steps = BLK // rows
    starts = [k * steps for k in range(blocks)]
    return pl.pallas_call(
        region_kernel,
        grid=(steps,),
        in_specs=[pl.BlockSpec((points, rows), lambda i, s=s: (0, s + i)) for s in starts]
        + [pl.BlockSpec((rows, wide), lambda i, s=s: (s + i, 0)) for s in starts]
        + [pl.BlockSpec((blocks, 1, wide), lambda i: (0, 0, 0))],
        out_specs=pl.BlockSpec((strips, points, wide // strips), lambda i: (0, 0, 0)),
        out_shape=jax.ShapeDtypeStruct((strips, points, wide // strips), bf16),
        scratch_shapes=[pltpu.VMEM((points, wide), f32)],
        compiler_params=pltpu.CompilerParams(vmem_limit_bytes=52 * 2**20),
        cost_estimate=pl.CostEstimate(
            flops=2 * points * cols * wide, bytes_accessed=2 * lmo.size, transcendentals=0
        ),
    )(*[pot] * blocks, *[lmo] * blocks, keep)


def place_kernel(z, parts, out):
    for m in range(NZ):
        total = jnp.sum(parts[:, m].astype(f32), axis=0)
        first = (z[0] + m) % NZ * NY
        for q in range(NY):
            out[pl.ds(first + q, 1)] = total[q * QP : (q + 1) * QP].astype(out.dtype)[None]


def sum_and_place(z, parts):
    whole = pl.BlockSpec(memory_space=pltpu.VMEM)
    return pl.pallas_call(
        place_kernel,
        in_specs=[pl.BlockSpec(memory_space=pltpu.SMEM), whole],
        out_specs=whole,
        out_shape=jax.ShapeDtypeStruct((NZ * NY, QP, BLK), bf16),
        cost_estimate=pl.CostEstimate(
            flops=parts.size, bytes_accessed=2 * parts.size, transcendentals=0
        ),
    )(z.reshape(1), parts)


def mask_kernel(sig, pv, out):
    cols = lax.broadcasted_iota(jnp.int32, (1, pv.shape[1]), 1)
    first = lax.axis_index("tile") * (pv.shape[1] // BLK)
    ids = first + lax.shift_right_logical(cols, BLK.bit_length() - 1)
    hit = ids == sig[:, 0:1]
    for i in range(1, sig.shape[1]):
        hit = hit | (ids == sig[:, i : i + 1])
    kept = jnp.where(hit, pv[...].astype(f32), 0.0).astype(out.dtype)
    for copy in range(out.shape[0]):
        out[copy] = kept


def masked_copies(sig, pv, n):
    whole = pl.BlockSpec(memory_space=pltpu.VMEM)
    return pl.pallas_call(
        mask_kernel,
        in_specs=[whole, whole],
        out_specs=whole,
        out_shape=jax.ShapeDtypeStruct((n,) + pv.shape, pv.dtype),
        cost_estimate=pl.CostEstimate(
            flops=pv.size, bytes_accessed=2 * (n + 1) * pv.size, transcendentals=0
        ),
    )(sig, pv)


def shards(pv, sig, density, core, smask, centers, widths, coords, lmo, dom):
    g, j = lax.axis_index("grid"), lax.axis_index("tile")
    z, y = g // NY, g % NY
    nblk = smask.shape[0]
    cols = pv.shape[1]
    ids = jnp.arange(nblk, dtype=jnp.int32)
    named = jnp.any(sig[0][:, None] == ids[None, :], axis=0).astype(f32)

    xy = masked_copies(sig, pv, NY)
    xy = lax.all_to_all(xy, "grid", 0, 0, tiled=True, axis_index_groups=Y_GROUPS)
    info = jnp.concatenate([named, coords.reshape(-1)])[None]
    piece = lax.dynamic_slice_in_dim(xy, y * BLK, BLK, 2)
    piece = piece.reshape(NT, NY, QP, BLK).transpose(1, 0, 2, 3).reshape(NY * BP, BLK)

    def product(buf, x, slot, row=0):
        rows = dot(x.reshape(-1, cols), density, 1, 1).astype(bf16)
        return lax.dynamic_update_slice(buf, rows.reshape(-1, 1, 16, BLK), (row, slot, 0, 0))

    info = permute_all(info, lambda a, b, c: (a, c // 2, 2 * b + c % 2))[0]
    info, xy = tie((info, xy))
    parts = product(jnp.zeros((NT, NZ, 16, BLK), bf16), xy, 0)
    up = down = xy
    for s in range(1, 4):
        up, down = along_z(up, 1), along_z(down, -1)
        parts = product(parts, up, NZ - s)
        parts = product(parts, down, s)
    up, down = along_z(up[:LEAD], 1), along_z(down[LEAD:], -1)
    parts = product(parts, up, 4)
    parts = product(parts, down, 4, 2 * LEAD)

    named = info[:nblk]
    pts = lax.dynamic_slice_in_dim(info[nblk:].reshape(3, BP), 16 * (j % 2) + QP * y, QP, 1)
    off = centers.reshape(3, nblk, 1, BLK) - pts.reshape(3, 1, QP, 1)
    coef = 1.0 / jnp.sqrt(jnp.sum(off * off, axis=0) + widths.reshape(nblk, 1, BLK))
    coef = coef * named[:, None, None]
    parts, coef, piece = tie((parts, coef, piece))
    piece = permute_all(piece, lambda a, b, c: (c, b, a))
    parts = lax.all_to_all(parts, "tile", 0, 0, tiled=True)
    term = sum_and_place(z, parts)
    term, piece = tie((term, piece))
    x_col = lax.all_gather(piece, "tile", axis=0, tiled=True)
    term = lax.all_to_all(term, "grid", 0, 0, tiled=True)

    weighted = (coef * term.astype(f32)).astype(bf16)
    screened = jnp.einsum("kj,jpa->kpa", smask.astype(bf16), weighted, preferred_element_type=f32)
    mixed = jnp.einsum("kpc,ac->kpa", screened.astype(bf16), core, preferred_element_type=f32)
    pot = (coef * mixed).astype(bf16)
    pot = lax.all_to_all(pot.reshape(NT, 4, QP, BLK), "tile", 0, 0, tiled=True)
    pot = pot.transpose(0, 2, 1, 3).reshape(NT * QP, cols)

    local_ids = 4 * j + jnp.arange(4, dtype=jnp.int32)
    in_dom = jnp.any(dom[:, :, None] == local_ids[None, None, :], axis=1).astype(jnp.int32)
    w = region_product(in_dom, pot, lmo)
    w = lax.all_to_all(w, "tile", 0, 0, tiled=True)
    w = jnp.sum(w.astype(f32), axis=0).astype(bf16)
    w, x_col = tie((w, x_col))
    w_all = spread(w, "grid", NZ * NY).reshape(-1, 256)
    return dot(w_all, x_col, 0, 0).astype(bf16)


def solution(mesh):
    in_specs = (
        P("grid", "tile"),
        P("grid", None),
        P("grid", "tile"),
        P(),
        P(),
        P(),
        P(),
        P(None, "grid"),
        P("tile", None),
        P(),
    )
    return jax.shard_map(
        shards, mesh=mesh, in_specs=in_specs, out_specs=P("tile", "grid"), check_vma=False
    )
```

```python
import jax
import jax.numpy as jnp
from jax import lax
from jax.experimental import pallas as pl
from jax.experimental.pallas import tpu as pltpu
from jax.sharding import PartitionSpec as P

NZ, NY, NT = 8, 4, 8
BP, BLK = 32, 512
QP = 4
LEAD = 1
bf16, f32 = jnp.bfloat16, jnp.float32
Y_GROUPS = [[z * NY + y for y in range(NY)] for z in range(NZ)]
tie = lax.optimization_barrier


def along_z(x, d):
    pairs = [(z * NY + y, (z + d) % NZ * NY + y) for z in range(NZ) for y in range(NY)]
    return lax.ppermute(x, "grid", pairs)


def permute_all(x, dest):
    pairs = []
    for z in range(NZ):
        for y in range(NY):
            for t in range(NT):
                a, b, c = dest(z, y, t)
                pairs.append(((z * NY + y) * NT + t, (a * NY + b) * NT + c))
    return lax.ppermute(x, ("grid", "tile"), pairs)


def spread(x, axis, n):
    copies = jnp.broadcast_to(x[None], (n,) + x.shape)
    return lax.all_to_all(copies, axis, 0, 0, tiled=True)


def dot(u, v, cu, cv):
    return lax.dot_general(u, v, (((cu,), (cv,)), ((), ())), preferred_element_type=f32)


def region_kernel(*refs):
    pots, lmos, keep, out, acc = refs[:4], refs[4:8], refs[8], refs[9], refs[10]
    step = pl.program_id(0)
    strips, _, width = out.shape

    @pl.when(step == 0)
    def _():
        acc[...] = jnp.zeros_like(acc)

    total = acc[...]
    for k in range(4):
        part = jnp.dot(pots[k][...], lmos[k][...], preferred_element_type=f32)
        total = total + jnp.where(keep[k] != 0, part, 0.0)
    acc[...] = total

    @pl.when(step == pl.num_programs(0) - 1)
    def _():
        for strip in range(strips):
            out[strip] = acc[:, strip * width : (strip + 1) * width].astype(out.dtype)


def region_product(in_dom, pot, lmo, rows=128):
    strips, blocks = in_dom.shape
    points, cols = pot.shape
    wide = lmo.shape[1]
    keep = jnp.repeat(in_dom.T, wide // strips, axis=1).reshape(blocks, 1, wide)
    steps = BLK // rows
    starts = [k * steps for k in range(blocks)]
    return pl.pallas_call(
        region_kernel,
        grid=(steps,),
        in_specs=[pl.BlockSpec((points, rows), lambda i, s=s: (0, s + i)) for s in starts]
        + [pl.BlockSpec((rows, wide), lambda i, s=s: (s + i, 0)) for s in starts]
        + [pl.BlockSpec((blocks, 1, wide), lambda i: (0, 0, 0))],
        out_specs=pl.BlockSpec((strips, points, wide // strips), lambda i: (0, 0, 0)),
        out_shape=jax.ShapeDtypeStruct((strips, points, wide // strips), bf16),
        scratch_shapes=[pltpu.VMEM((points, wide), f32)],
        compiler_params=pltpu.CompilerParams(vmem_limit_bytes=52 * 2**20),
        cost_estimate=pl.CostEstimate(
            flops=2 * points * cols * wide, bytes_accessed=2 * lmo.size, transcendentals=0
        ),
    )(*[pot] * blocks, *[lmo] * blocks, keep)


def place_kernel(z, parts, late, out):
    for m in range(NZ):
        part = late[:, 0] if m == 4 else parts[:, m - (m > 4)]
        total = jnp.sum(part.astype(f32), axis=0)
        first = (z[0] + m) % NZ * NY
        for q in range(NY):
            out[pl.ds(first + q, 1)] = total[q * QP : (q + 1) * QP].astype(out.dtype)[None]


def sum_and_place(z, parts, late):
    whole = pl.BlockSpec(memory_space=pltpu.VMEM)
    return pl.pallas_call(
        place_kernel,
        in_specs=[pl.BlockSpec(memory_space=pltpu.SMEM), whole, whole],
        out_specs=whole,
        out_shape=jax.ShapeDtypeStruct((NZ * NY, QP, BLK), bf16),
        cost_estimate=pl.CostEstimate(
            flops=parts.size, bytes_accessed=2 * parts.size, transcendentals=0
        ),
    )(z.reshape(1), parts, late)


def mask_kernel(sig, pv, out):
    cols = lax.broadcasted_iota(jnp.int32, (1, pv.shape[1]), 1)
    first = lax.axis_index("tile") * (pv.shape[1] // BLK)
    ids = first + lax.shift_right_logical(cols, BLK.bit_length() - 1)
    hit = ids == sig[:, 0:1]
    for i in range(1, sig.shape[1]):
        hit = hit | (ids == sig[:, i : i + 1])
    kept = jnp.where(hit, pv[...].astype(f32), 0.0).astype(out.dtype)
    for copy in range(out.shape[0]):
        out[copy] = kept


def masked_copies(sig, pv, n):
    whole = pl.BlockSpec(memory_space=pltpu.VMEM)
    return pl.pallas_call(
        mask_kernel,
        in_specs=[whole, whole],
        out_specs=whole,
        out_shape=jax.ShapeDtypeStruct((n,) + pv.shape, pv.dtype),
        cost_estimate=pl.CostEstimate(
            flops=pv.size, bytes_accessed=2 * (n + 1) * pv.size, transcendentals=0
        ),
    )(sig, pv)


def shards(pv, sig, density, core, smask, centers, widths, coords, lmo, dom):
    g, j = lax.axis_index("grid"), lax.axis_index("tile")
    z, y = g // NY, g % NY
    nblk = smask.shape[0]
    cols = pv.shape[1]
    ids = jnp.arange(nblk, dtype=jnp.int32)
    named = jnp.any(sig[0][:, None] == ids[None, :], axis=0).astype(f32)

    xy = masked_copies(sig, pv, NY)
    xy = lax.all_to_all(xy, "grid", 0, 0, tiled=True, axis_index_groups=Y_GROUPS)
    info = jnp.concatenate([named, coords.reshape(-1)])[None]
    piece = lax.dynamic_slice_in_dim(xy, y * BLK, BLK, 2)
    piece = piece.reshape(NT, NY, QP, BLK).transpose(1, 0, 2, 3).reshape(NY * BP, BLK)

    def product(buf, x, slot, row=0):
        rows = dot(x.reshape(-1, cols), density, 1, 1).astype(bf16)
        return lax.dynamic_update_slice(buf, rows.reshape(-1, 1, 16, BLK), (row, slot, 0, 0))

    info = permute_all(info, lambda a, b, c: (a, c // 2, 2 * b + c % 2))[0]
    info, xy = tie((info, xy))
    parts = product(jnp.zeros((NT, NZ - 1, 16, BLK), bf16), xy, 0)
    up = down = xy
    for s in range(1, 4):
        up, down = along_z(up, 1), along_z(down, -1)
        parts = product(parts, up, NZ - s - 1)
        parts = product(parts, down, s)
    up, down = along_z(up[:LEAD], 1), along_z(down[LEAD:], -1)
    over_tile = lambda v: lax.all_to_all(v, "tile", 0, 0, tiled=True)
    parts = over_tile(parts)
    late = product(jnp.zeros((NT, 1, 16, BLK), bf16), up, 0)
    late = product(late, down, 0, 2 * LEAD)

    named = info[:nblk]
    pts = lax.dynamic_slice_in_dim(info[nblk:].reshape(3, BP), 16 * (j % 2) + QP * y, QP, 1)
    off = centers.reshape(3, nblk, 1, BLK) - pts.reshape(3, 1, QP, 1)
    coef = 1.0 / jnp.sqrt(jnp.sum(off * off, axis=0) + widths.reshape(nblk, 1, BLK))
    coef = coef * named[:, None, None]
    late, coef, piece, parts = tie((late, coef, piece, parts))
    piece = permute_all(piece, lambda a, b, c: (c, b, a))
    term = sum_and_place(z, parts, over_tile(late))
    term, piece = tie((term, piece))
    x_col = lax.all_gather(piece, "tile", axis=0, tiled=True)
    term = lax.all_to_all(term, "grid", 0, 0, tiled=True)

    weighted = (coef * term.astype(f32)).astype(bf16)
    screened = jnp.einsum("kj,jpa->kpa", smask.astype(bf16), weighted, preferred_element_type=f32)
    mixed = jnp.einsum("kpc,ac->kpa", screened.astype(bf16), core, preferred_element_type=f32)
    pot = (coef * mixed).astype(bf16)
    pot = lax.all_to_all(pot.reshape(NT, 4, QP, BLK), "tile", 0, 0, tiled=True)
    pot = pot.transpose(0, 2, 1, 3).reshape(NT * QP, cols)

    local_ids = 4 * j + jnp.arange(4, dtype=jnp.int32)
    in_dom = jnp.any(dom[:, :, None] == local_ids[None, None, :], axis=1).astype(jnp.int32)
    w = region_product(in_dom, pot, lmo)
    w = lax.all_to_all(w, "tile", 0, 0, tiled=True)
    w = jnp.sum(w.astype(f32), axis=0).astype(bf16)
    w, x_col = tie((w, x_col))
    w_all = spread(w, "grid", NZ * NY).reshape(-1, 256)
    return dot(w_all, x_col, 0, 0).astype(bf16)


def solution(mesh):
    in_specs = (
        P("grid", "tile"),
        P("grid", None),
        P("grid", "tile"),
        P(),
        P(),
        P(),
        P(),
        P(None, "grid"),
        P("tile", None),
        P(),
    )
    return jax.shard_map(
        shards, mesh=mesh, in_specs=in_specs, out_specs=P("tile", "grid"), check_vma=False
    )
```

```python
import jax
import jax.numpy as jnp
from jax import lax
from jax.experimental import pallas as pl
from jax.experimental.pallas import tpu as pltpu
from jax.sharding import PartitionSpec as P

NZ, NY, NT = 8, 4, 8
BP, BLK = 32, 512
QP = 4
LEAD = 1
bf16, f32 = jnp.bfloat16, jnp.float32
Y_GROUPS = [[z * NY + y for y in range(NY)] for z in range(NZ)]
tie = lax.optimization_barrier


def along_z(x, d):
    pairs = [(z * NY + y, (z + d) % NZ * NY + y) for z in range(NZ) for y in range(NY)]
    return lax.ppermute(x, "grid", pairs)


def permute_all(x, dest):
    pairs = []
    for z in range(NZ):
        for y in range(NY):
            for t in range(NT):
                a, b, c = dest(z, y, t)
                pairs.append(((z * NY + y) * NT + t, (a * NY + b) * NT + c))
    return lax.ppermute(x, ("grid", "tile"), pairs)


def spread(x, axis, n):
    copies = jnp.broadcast_to(x[None], (n,) + x.shape)
    return lax.all_to_all(copies, axis, 0, 0, tiled=True)


def dot(u, v, cu, cv):
    return lax.dot_general(u, v, (((cu,), (cv,)), ((), ())), preferred_element_type=f32)


def region_kernel(*refs):
    pots, lmos, keep, out, acc = refs[:4], refs[4:8], refs[8], refs[9], refs[10]
    step = pl.program_id(0)
    strips, _, width = out.shape

    @pl.when(step == 0)
    def _():
        acc[...] = jnp.zeros_like(acc)

    total = acc[...]
    for k in range(4):
        part = jnp.dot(pots[k][...], lmos[k][...], preferred_element_type=f32)
        total = total + jnp.where(keep[k] != 0, part, 0.0)
    acc[...] = total

    @pl.when(step == pl.num_programs(0) - 1)
    def _():
        for strip in range(strips):
            out[strip] = acc[:, strip * width : (strip + 1) * width].astype(out.dtype)


def region_product(in_dom, pot, lmo, rows=128):
    strips, blocks = in_dom.shape
    points, cols = pot.shape
    wide = lmo.shape[1]
    keep = jnp.repeat(in_dom.T, wide // strips, axis=1).reshape(blocks, 1, wide)
    steps = BLK // rows
    starts = [k * steps for k in range(blocks)]
    return pl.pallas_call(
        region_kernel,
        grid=(steps,),
        in_specs=[pl.BlockSpec((points, rows), lambda i, s=s: (0, s + i)) for s in starts]
        + [pl.BlockSpec((rows, wide), lambda i, s=s: (s + i, 0)) for s in starts]
        + [pl.BlockSpec((blocks, 1, wide), lambda i: (0, 0, 0))],
        out_specs=pl.BlockSpec((strips, points, wide // strips), lambda i: (0, 0, 0)),
        out_shape=jax.ShapeDtypeStruct((strips, points, wide // strips), bf16),
        scratch_shapes=[pltpu.VMEM((points, wide), f32)],
        compiler_params=pltpu.CompilerParams(vmem_limit_bytes=52 * 2**20),
        cost_estimate=pl.CostEstimate(
            flops=2 * points * cols * wide, bytes_accessed=2 * lmo.size, transcendentals=0
        ),
    )(*[pot] * blocks, *[lmo] * blocks, keep)


def place_kernel(z, *refs):
    quarters, out = refs[:4], refs[4]
    for m in range(NZ):
        total = sum(jnp.sum(part[:, m].astype(f32), axis=0) for part in quarters)
        first = (z[0] + m) % NZ * NY
        for q in range(NY):
            out[pl.ds(first + q, 1)] = total[q * QP : (q + 1) * QP].astype(out.dtype)[None]


def sum_and_place(z, parts):
    block = (NT // 4,) + parts.shape[1:]
    shape = (NZ * NY, QP, BLK)
    return pl.pallas_call(
        place_kernel,
        grid=(1,),
        in_specs=[pl.BlockSpec(memory_space=pltpu.SMEM)]
        + [pl.BlockSpec(block, lambda i, k=k: (k, 0, 0, 0)) for k in range(4)],
        out_specs=pl.BlockSpec(shape, lambda i: (0, 0, 0)),
        out_shape=jax.ShapeDtypeStruct(shape, bf16),
        cost_estimate=pl.CostEstimate(
            flops=parts.size, bytes_accessed=2 * parts.size, transcendentals=0
        ),
    )(z.reshape(1), *[parts] * 4)


def last_kernel(*refs):
    n = len(refs) // 2
    total = 0.0
    for w, x in zip(refs[:n], refs[n : 2 * n]):
        total = total + dot(w[...], x[...], 0, 0)
    refs[-1][...] = total.astype(refs[-1].dtype)


def last_product(w, x, streams=4):
    rows = w.shape[0] // streams
    shape = (w.shape[1], x.shape[1])
    at = lambda v, k: pl.BlockSpec((rows, v.shape[1]), lambda i: (k, 0))
    return pl.pallas_call(
        last_kernel,
        grid=(1,),
        in_specs=[at(v, k) for v in (w, x) for k in range(streams)],
        out_specs=pl.BlockSpec(shape, lambda i: (0, 0)),
        out_shape=jax.ShapeDtypeStruct(shape, bf16),
        cost_estimate=pl.CostEstimate(
            flops=2 * w.size * x.shape[1], bytes_accessed=2 * (w.size + x.size), transcendentals=0
        ),
    )(*[w] * streams, *[x] * streams)


def mask_kernel(sig, pv, out):
    cols = lax.broadcasted_iota(jnp.int32, (1, pv.shape[1]), 1)
    first = lax.axis_index("tile") * (pv.shape[1] // BLK)
    ids = first + lax.shift_right_logical(cols, BLK.bit_length() - 1)
    hit = ids == sig[:, 0:1]
    for i in range(1, sig.shape[1]):
        hit = hit | (ids == sig[:, i : i + 1])
    kept = jnp.where(hit, pv[...].astype(f32), 0.0).astype(out.dtype)
    for copy in range(out.shape[0]):
        out[copy] = kept


def masked_copies(sig, pv, n):
    whole = pl.BlockSpec(memory_space=pltpu.VMEM)
    return pl.pallas_call(
        mask_kernel,
        in_specs=[whole, whole],
        out_specs=whole,
        out_shape=jax.ShapeDtypeStruct((n,) + pv.shape, pv.dtype),
        cost_estimate=pl.CostEstimate(
            flops=pv.size, bytes_accessed=2 * (n + 1) * pv.size, transcendentals=0
        ),
    )(sig, pv)


def shards(pv, sig, density, core, smask, centers, widths, coords, lmo, dom):
    g, j = lax.axis_index("grid"), lax.axis_index("tile")
    z, y = g // NY, g % NY
    nblk = smask.shape[0]
    cols = pv.shape[1]
    ids = jnp.arange(nblk, dtype=jnp.int32)
    named = jnp.any(sig[0][:, None] == ids[None, :], axis=0).astype(f32)

    xy = masked_copies(sig, pv, NY)
    xy = lax.all_to_all(xy, "grid", 0, 0, tiled=True, axis_index_groups=Y_GROUPS)
    info = jnp.concatenate([named, coords.reshape(-1)])[None]
    piece = lax.dynamic_slice_in_dim(xy, y * BLK, BLK, 2)
    piece = piece.reshape(NT, NY, QP, BLK).transpose(1, 0, 2, 3).reshape(NY * BP, BLK)

    def product(buf, x, slot, row=0):
        rows = dot(x.reshape(-1, cols), density, 1, 1).astype(bf16)
        return lax.dynamic_update_slice(buf, rows.reshape(-1, 1, 16, BLK), (row, slot, 0, 0))

    info = permute_all(info, lambda a, b, c: (a, c // 2, 2 * b + c % 2))[0]
    info, xy = tie((info, xy))
    parts = product(jnp.zeros((NT, NZ, 16, BLK), bf16), xy, 0)
    up = down = xy
    for s in range(1, 4):
        up, down = along_z(up, 1), along_z(down, -1)
        parts = product(parts, up, NZ - s)
        parts = product(parts, down, s)
    up, down = along_z(up[:LEAD], 1), along_z(down[LEAD:], -1)
    parts = product(parts, up, 4)
    parts = product(parts, down, 4, 2 * LEAD)

    named = info[:nblk]
    pts = lax.dynamic_slice_in_dim(info[nblk:].reshape(3, BP), 16 * (j % 2) + QP * y, QP, 1)
    off = centers.reshape(3, nblk, 1, BLK) - pts.reshape(3, 1, QP, 1)
    coef = 1.0 / jnp.sqrt(jnp.sum(off * off, axis=0) + widths.reshape(nblk, 1, BLK))
    coef = coef * named[:, None, None]
    parts, coef, piece = tie((parts, coef, piece))
    piece = permute_all(piece, lambda a, b, c: (c, b, a))
    parts = lax.all_to_all(parts, "tile", 0, 0, tiled=True)
    term = sum_and_place(z, parts)
    term, piece = tie((term, piece))
    x_col = lax.all_gather(piece, "tile", axis=0, tiled=True)
    term = lax.all_to_all(term, "grid", 0, 0, tiled=True)

    weighted = (coef * term.astype(f32)).astype(bf16)
    screened = jnp.einsum("kj,jpa->kpa", smask.astype(bf16), weighted, preferred_element_type=f32)
    mixed = jnp.einsum("kpc,ac->kpa", screened.astype(bf16), core, preferred_element_type=f32)
    pot = (coef * mixed).astype(bf16)
    pot = lax.all_to_all(pot.reshape(NT, 4, QP, BLK), "tile", 0, 0, tiled=True)
    pot = pot.transpose(0, 2, 1, 3).reshape(NT * QP, cols)

    local_ids = 4 * j + jnp.arange(4, dtype=jnp.int32)
    in_dom = jnp.any(dom[:, :, None] == local_ids[None, None, :], axis=1).astype(jnp.int32)
    w = region_product(in_dom, pot, lmo)
    w = lax.all_to_all(w, "tile", 0, 0, tiled=True)
    w = jnp.sum(w.astype(f32), axis=0).astype(bf16)
    w, x_col = tie((w, x_col))
    w_all = spread(w, "grid", NZ * NY).reshape(-1, 256)
    return last_product(w_all, x_col)


def solution(mesh):
    in_specs = (
        P("grid", "tile"),
        P("grid", None),
        P("grid", "tile"),
        P(),
        P(),
        P(),
        P(),
        P(None, "grid"),
        P("tile", None),
        P(),
    )
    return jax.shard_map(
        shards, mesh=mesh, in_specs=in_specs, out_specs=P("tile", "grid"), check_vma=False
    )
```

```python
import jax
import jax.numpy as jnp
from jax import lax
from jax.experimental import pallas as pl
from jax.experimental.pallas import tpu as pltpu
from jax.sharding import PartitionSpec as P

NZ, NY, NT = 8, 4, 8
BP, BLK = 32, 512
QP = 4
LEAD = 1
bf16, f32 = jnp.bfloat16, jnp.float32
Y_GROUPS = [[z * NY + y for y in range(NY)] for z in range(NZ)]
tie = lax.optimization_barrier


def along_z(x, d):
    pairs = [(z * NY + y, (z + d) % NZ * NY + y) for z in range(NZ) for y in range(NY)]
    return lax.ppermute(x, "grid", pairs)


def permute_all(x, dest):
    pairs = []
    for z in range(NZ):
        for y in range(NY):
            for t in range(NT):
                a, b, c = dest(z, y, t)
                pairs.append(((z * NY + y) * NT + t, (a * NY + b) * NT + c))
    return lax.ppermute(x, ("grid", "tile"), pairs)


def spread(x, axis, n):
    copies = jnp.broadcast_to(x[None], (n,) + x.shape)
    return lax.all_to_all(copies, axis, 0, 0, tiled=True)


def dot(u, v, cu, cv):
    return lax.dot_general(u, v, (((cu,), (cv,)), ((), ())), preferred_element_type=f32)


def region_kernel(*refs):
    pots, lmos, keep, out, acc = refs[:4], refs[4:8], refs[8], refs[9], refs[10]
    step = pl.program_id(0)
    strips, _, width = out.shape

    @pl.when(step == 0)
    def _():
        acc[...] = jnp.zeros_like(acc)

    total = acc[...]
    for k in range(4):
        part = jnp.dot(pots[k][...], lmos[k][...], preferred_element_type=f32)
        total = total + jnp.where(keep[k] != 0, part, 0.0)
    acc[...] = total

    @pl.when(step == pl.num_programs(0) - 1)
    def _():
        for strip in range(strips):
            out[strip] = acc[:, strip * width : (strip + 1) * width].astype(out.dtype)


def region_product(in_dom, pot, lmo, rows=128):
    strips, blocks = in_dom.shape
    points, cols = pot.shape
    wide = lmo.shape[1]
    keep = jnp.repeat(in_dom.T, wide // strips, axis=1).reshape(blocks, 1, wide)
    steps = BLK // rows
    starts = [k * steps for k in range(blocks)]
    return pl.pallas_call(
        region_kernel,
        grid=(steps,),
        in_specs=[pl.BlockSpec((points, rows), lambda i, s=s: (0, s + i)) for s in starts]
        + [pl.BlockSpec((rows, wide), lambda i, s=s: (s + i, 0)) for s in starts]
        + [pl.BlockSpec((blocks, 1, wide), lambda i: (0, 0, 0))],
        out_specs=pl.BlockSpec((strips, points, wide // strips), lambda i: (0, 0, 0)),
        out_shape=jax.ShapeDtypeStruct((strips, points, wide // strips), bf16),
        scratch_shapes=[pltpu.VMEM((points, wide), f32)],
        compiler_params=pltpu.CompilerParams(vmem_limit_bytes=52 * 2**20),
        cost_estimate=pl.CostEstimate(
            flops=2 * points * cols * wide, bytes_accessed=2 * lmo.size, transcendentals=0
        ),
    )(*[pot] * blocks, *[lmo] * blocks, keep)


def place_kernel(parts, out):
    z = lax.axis_index("grid") // NY
    for m in range(NZ):
        total = jnp.sum(parts[:, m].astype(f32), axis=0)
        first = (z + m) % NZ * NY
        for q in range(NY):
            out[pl.ds(first + q, 1)] = total[q * QP : (q + 1) * QP].astype(out.dtype)[None]


def sum_and_place(parts):
    whole = pl.BlockSpec(memory_space=pltpu.VMEM)
    return pl.pallas_call(
        place_kernel,
        in_specs=[whole],
        out_specs=whole,
        out_shape=jax.ShapeDtypeStruct((NZ * NY, QP, BLK), bf16),
        cost_estimate=pl.CostEstimate(
            flops=parts.size, bytes_accessed=2 * parts.size, transcendentals=0
        ),
    )(parts)


def mask_kernel(sig, pv, out):
    cols = lax.broadcasted_iota(jnp.int32, (1, pv.shape[1]), 1)
    first = lax.axis_index("tile") * (pv.shape[1] // BLK)
    ids = first + lax.shift_right_logical(cols, BLK.bit_length() - 1)
    hit = ids == sig[:, 0:1]
    for i in range(1, sig.shape[1]):
        hit = hit | (ids == sig[:, i : i + 1])
    kept = jnp.where(hit, pv[...].astype(f32), 0.0).astype(out.dtype)
    for copy in range(out.shape[0]):
        out[copy] = kept


def masked_copies(sig, pv, n):
    whole = pl.BlockSpec(memory_space=pltpu.VMEM)
    return pl.pallas_call(
        mask_kernel,
        in_specs=[whole, whole],
        out_specs=whole,
        out_shape=jax.ShapeDtypeStruct((n,) + pv.shape, pv.dtype),
        cost_estimate=pl.CostEstimate(
            flops=pv.size, bytes_accessed=2 * (n + 1) * pv.size, transcendentals=0
        ),
    )(sig, pv)


def shards(pv, sig, density, core, smask, centers, widths, coords, lmo, dom):
    g, j = lax.axis_index("grid"), lax.axis_index("tile")
    z, y = g // NY, g % NY
    nblk = smask.shape[0]
    cols = pv.shape[1]
    ids = jnp.arange(nblk, dtype=jnp.int32)
    named = jnp.any(sig[0][:, None] == ids[None, :], axis=0).astype(f32)

    xy = masked_copies(sig, pv, NY)
    xy = lax.all_to_all(xy, "grid", 0, 0, tiled=True, axis_index_groups=Y_GROUPS)
    info = jnp.concatenate([named, coords.reshape(-1)])[None]
    piece = lax.dynamic_slice_in_dim(xy, y * BLK, BLK, 2)
    piece = piece.reshape(NT, NY, QP, BLK).transpose(1, 0, 2, 3).reshape(NY * BP, BLK)

    def product(buf, x, slot, row=0):
        rows = dot(x.reshape(-1, cols), density, 1, 1).astype(bf16)
        return lax.dynamic_update_slice(buf, rows.reshape(-1, 1, 16, BLK), (row, slot, 0, 0))

    info = permute_all(info, lambda a, b, c: (a, c // 2, 2 * b + c % 2))[0]
    info, xy = tie((info, xy))
    parts = product(jnp.zeros((NT, NZ, 16, BLK), bf16), xy, 0)
    up = down = xy
    for s in range(1, 4):
        up, down = along_z(up, 1), along_z(down, -1)
        parts = product(parts, up, NZ - s)
        parts = product(parts, down, s)
    up, down = along_z(up[:LEAD], 1), along_z(down[LEAD:], -1)
    parts = product(parts, up, 4)
    parts = product(parts, down, 4, 2 * LEAD)

    named = info[:nblk]
    pts = lax.dynamic_slice_in_dim(info[nblk:].reshape(3, BP), 16 * (j % 2) + QP * y, QP, 1)
    off = centers.reshape(3, nblk, 1, BLK) - pts.reshape(3, 1, QP, 1)
    coef = 1.0 / jnp.sqrt(jnp.sum(off * off, axis=0) + widths.reshape(nblk, 1, BLK))
    coef = coef * named[:, None, None]
    parts, coef, piece = tie((parts, coef, piece))
    piece = permute_all(piece, lambda a, b, c: (c, b, a))
    parts = lax.all_to_all(parts, "tile", 0, 0, tiled=True)
    term = sum_and_place(parts)
    term, piece = tie((term, piece))
    x_col = lax.all_gather(piece, "tile", axis=0, tiled=True)
    term = lax.all_to_all(term, "grid", 0, 0, tiled=True)

    weighted = (coef * term.astype(f32)).astype(bf16)
    screened = jnp.einsum("kj,jpa->kpa", smask.astype(bf16), weighted, preferred_element_type=f32)
    mixed = jnp.einsum("kpc,ac->kpa", screened.astype(bf16), core, preferred_element_type=f32)
    pot = (coef * mixed).astype(bf16)
    pot = lax.all_to_all(pot.reshape(NT, 4, QP, BLK), "tile", 0, 0, tiled=True)
    pot = pot.transpose(0, 2, 1, 3).reshape(NT * QP, cols)

    local_ids = 4 * j + jnp.arange(4, dtype=jnp.int32)
    in_dom = jnp.any(dom[:, :, None] == local_ids[None, None, :], axis=1).astype(jnp.int32)
    w = region_product(in_dom, pot, lmo)
    w = lax.all_to_all(w, "tile", 0, 0, tiled=True)
    w = jnp.sum(w.astype(f32), axis=0).astype(bf16)
    w, x_col = tie((w, x_col))
    w_all = spread(w, "grid", NZ * NY).reshape(-1, 256)
    return dot(w_all, x_col, 0, 0).astype(bf16)


def solution(mesh):
    in_specs = (
        P("grid", "tile"),
        P("grid", None),
        P("grid", "tile"),
        P(),
        P(),
        P(),
        P(),
        P(None, "grid"),
        P("tile", None),
        P(),
    )
    return jax.shard_map(
        shards, mesh=mesh, in_specs=in_specs, out_specs=P("tile", "grid"), check_vma=False
    )
```

```python
import jax
import jax.numpy as jnp
from jax import lax
from jax.experimental import pallas as pl
from jax.experimental.pallas import tpu as pltpu
from jax.sharding import PartitionSpec as P

NZ, NY, NT = 8, 4, 8
BP, BLK = 32, 512
QP = 4
LEAD = 1
bf16, f32 = jnp.bfloat16, jnp.float32
Y_GROUPS = [[z * NY + y for y in range(NY)] for z in range(NZ)]
tie = lax.optimization_barrier


def along_z(x, d):
    pairs = [(z * NY + y, (z + d) % NZ * NY + y) for z in range(NZ) for y in range(NY)]
    return lax.ppermute(x, "grid", pairs)


def permute_all(x, dest):
    pairs = []
    for z in range(NZ):
        for y in range(NY):
            for t in range(NT):
                a, b, c = dest(z, y, t)
                pairs.append(((z * NY + y) * NT + t, (a * NY + b) * NT + c))
    return lax.ppermute(x, ("grid", "tile"), pairs)


def spread(x, axis, n):
    copies = jnp.broadcast_to(x[None], (n,) + x.shape)
    return lax.all_to_all(copies, axis, 0, 0, tiled=True)


def dot(u, v, cu, cv):
    return lax.dot_general(u, v, (((cu,), (cv,)), ((), ())), preferred_element_type=f32)


def region_kernel(*refs):
    pots, lmos, keep, out, acc = refs[:4], refs[4:8], refs[8], refs[9], refs[10]
    step = pl.program_id(0)
    strips, _, width = out.shape

    @pl.when(step == 0)
    def _():
        acc[...] = jnp.zeros_like(acc)

    total = acc[...]
    for k in range(4):
        part = jnp.dot(pots[k][...], lmos[k][...], preferred_element_type=f32)
        total = total + jnp.where(keep[k] != 0, part, 0.0)
    acc[...] = total

    @pl.when(step == pl.num_programs(0) - 1)
    def _():
        for strip in range(strips):
            out[strip] = acc[:, strip * width : (strip + 1) * width].astype(out.dtype)


def region_product(in_dom, pot, lmo, rows=128):
    strips, blocks = in_dom.shape
    points, cols = pot.shape
    wide = lmo.shape[1]
    keep = jnp.repeat(in_dom.T, wide // strips, axis=1).reshape(blocks, 1, wide)
    steps = BLK // rows
    starts = [k * steps for k in range(blocks)]
    return pl.pallas_call(
        region_kernel,
        grid=(steps,),
        in_specs=[pl.BlockSpec((points, rows), lambda i, s=s: (0, s + i)) for s in starts]
        + [pl.BlockSpec((rows, wide), lambda i, s=s: (s + i, 0)) for s in starts]
        + [pl.BlockSpec((blocks, 1, wide), lambda i: (0, 0, 0))],
        out_specs=pl.BlockSpec((strips, points, wide // strips), lambda i: (0, 0, 0)),
        out_shape=jax.ShapeDtypeStruct((strips, points, wide // strips), bf16),
        scratch_shapes=[pltpu.VMEM((points, wide), f32)],
        compiler_params=pltpu.CompilerParams(vmem_limit_bytes=52 * 2**20),
        cost_estimate=pl.CostEstimate(
            flops=2 * points * cols * wide, bytes_accessed=2 * lmo.size, transcendentals=0
        ),
    )(*[pot] * blocks, *[lmo] * blocks, keep)


def place_kernel(parts, out):
    z = lax.axis_index("grid") // NY
    for m in range(NZ):
        total = jnp.sum(parts[:, m].astype(f32), axis=0)
        first = (z + m) % NZ * NY
        for q in range(NY):
            out[pl.ds(first + q, 1)] = total[q * QP : (q + 1) * QP].astype(out.dtype)[None]


def sum_and_place(parts):
    whole = pl.BlockSpec(memory_space=pltpu.VMEM)
    return pl.pallas_call(
        place_kernel,
        in_specs=[whole],
        out_specs=whole,
        out_shape=jax.ShapeDtypeStruct((NZ * NY, QP, BLK), bf16),
        cost_estimate=pl.CostEstimate(
            flops=parts.size, bytes_accessed=2 * parts.size, transcendentals=0
        ),
    )(parts)


def mask_kernel(sig, pv, out):
    cols = lax.broadcasted_iota(jnp.int32, (1, pv.shape[1]), 1)
    first = lax.axis_index("tile") * (pv.shape[1] // BLK)
    ids = first + lax.shift_right_logical(cols, BLK.bit_length() - 1)
    hit = ids == sig[:, 0:1]
    for i in range(1, sig.shape[1]):
        hit = hit | (ids == sig[:, i : i + 1])
    kept = jnp.where(hit, pv[...].astype(f32), 0.0).astype(out.dtype)
    for copy in range(out.shape[0]):
        out[copy] = kept


def masked_copies(sig, pv, n):
    whole = pl.BlockSpec(memory_space=pltpu.VMEM)
    return pl.pallas_call(
        mask_kernel,
        in_specs=[whole, whole],
        out_specs=whole,
        out_shape=jax.ShapeDtypeStruct((n,) + pv.shape, pv.dtype),
        cost_estimate=pl.CostEstimate(
            flops=pv.size, bytes_accessed=2 * (n + 1) * pv.size, transcendentals=0
        ),
    )(sig, pv)


def shards(pv, sig, density, core, smask, centers, widths, coords, lmo, dom):
    g, j = lax.axis_index("grid"), lax.axis_index("tile")
    z, y = g // NY, g % NY
    nblk = smask.shape[0]
    cols = pv.shape[1]
    ids = jnp.arange(nblk, dtype=jnp.int32)
    named = jnp.any(sig[0][:, None] == ids[None, :], axis=0).astype(f32)

    xy = masked_copies(sig, pv, NY)
    xy = lax.all_to_all(xy, "grid", 0, 0, tiled=True, axis_index_groups=Y_GROUPS)
    info = jnp.concatenate([named, coords.reshape(-1)])[None]
    piece = lax.dynamic_slice_in_dim(xy, y * BLK, BLK, 2)
    piece = piece.reshape(NT, NY, QP, BLK).transpose(1, 0, 2, 3).reshape(NY * BP, BLK)

    def product(buf, x, slot, row=0):
        rows = dot(x.reshape(-1, cols), density, 1, 1).astype(bf16)
        return lax.dynamic_update_slice(buf, rows.reshape(-1, 1, 16, BLK), (row, slot, 0, 0))

    info = permute_all(info, lambda a, b, c: (a, c // 2, 2 * b + c % 2))[0]
    info, xy = tie((info, xy))
    parts = product(jnp.zeros((NT, NZ, 16, BLK), bf16), xy, 0)
    up = down = xy
    for s in range(1, 4):
        up, down = along_z(up, 1), along_z(down, -1)
        parts = product(parts, up, NZ - s)
        parts = product(parts, down, s)
    up, down = along_z(up[:LEAD], 1), along_z(down[LEAD:], -1)
    parts = product(parts, up, 4)
    parts = product(parts, down, 4, 2 * LEAD)

    named = info[:nblk]
    pts = lax.dynamic_slice_in_dim(info[nblk:].reshape(3, BP), 16 * (j % 2) + QP * y, QP, 1)
    off = centers.reshape(3, nblk, 1, BLK) - pts.reshape(3, 1, QP, 1)
    coef = 1.0 / jnp.sqrt(jnp.sum(off * off, axis=0) + widths.reshape(nblk, 1, BLK))
    coef = coef * named[:, None, None]
    parts, coef, piece = tie((parts, coef, piece))
    parts = lax.all_to_all(parts, "tile", 0, 0, tiled=True)
    term = sum_and_place(parts)
    term, piece = tie((term, piece))
    piece = permute_all(piece, lambda a, b, c: (c, b, a))
    x_col = lax.all_gather(piece, "tile", axis=0, tiled=True)
    term = lax.all_to_all(term, "grid", 0, 0, tiled=True)

    weighted = (coef * term.astype(f32)).astype(bf16)
    screened = jnp.einsum("kj,jpa->kpa", smask.astype(bf16), weighted, preferred_element_type=f32)
    mixed = jnp.einsum("kpc,ac->kpa", screened.astype(bf16), core, preferred_element_type=f32)
    pot = (coef * mixed).astype(bf16)
    pot = lax.all_to_all(pot.reshape(NT, 4, QP, BLK), "tile", 0, 0, tiled=True)
    pot = pot.transpose(0, 2, 1, 3).reshape(NT * QP, cols)

    local_ids = 4 * j + jnp.arange(4, dtype=jnp.int32)
    in_dom = jnp.any(dom[:, :, None] == local_ids[None, None, :], axis=1).astype(jnp.int32)
    w = region_product(in_dom, pot, lmo)
    w = lax.all_to_all(w, "tile", 0, 0, tiled=True)
    w = jnp.sum(w.astype(f32), axis=0).astype(bf16)
    w, x_col = tie((w, x_col))
    w_all = spread(w, "grid", NZ * NY).reshape(-1, 256)
    return dot(w_all, x_col, 0, 0).astype(bf16)


def solution(mesh):
    in_specs = (
        P("grid", "tile"),
        P("grid", None),
        P("grid", "tile"),
        P(),
        P(),
        P(),
        P(),
        P(None, "grid"),
        P("tile", None),
        P(),
    )
    return jax.shard_map(
        shards, mesh=mesh, in_specs=in_specs, out_specs=P("tile", "grid"), check_vma=False
    )
```
